256 devices in a mesh: group: 16 (over y_lo, z), fsdp: 16 (over x, y_hi, core).
Axes of the slice: x: 4, y: 4 (y_hi: 2, y_lo: 2; y = y_hi * 2 + y_lo), z: 8, core: 2. Of those that a mesh axis runs over, the one named last changes fastest.
Arguments:
- activations: bfloat16 [65536, 2560], P(('group', 'fsdp')), may hold values from -24 to 24
- cotangent: bfloat16 [65536, 2560], P(('group', 'fsdp')), may hold values from -6 to 6
- token_ids: int32 [65536], P(('group', 'fsdp')), may hold values from -100 to 31999, as said below
- step_count: int32 [1], replicated, may hold values from 0 to 7
- master: float32 [16, 2560, 2560], P('group', 'fsdp'), may hold values from -0.12 to 0.12
- first_moment: bfloat16 [16, 2560, 2560], P('group', 'fsdp'), may hold values from -150 to 150
- second_moment: bfloat16 [16, 2560, 2560], P('group', 'fsdp'), may hold values from 200 to 3200
Outputs:
- output: bfloat16 [65536, 2560], P(('group', 'fsdp'))
- act_grad: bfloat16 [65536, 2560], P(('group', 'fsdp'))
- new_master: float32 [16, 2560, 2560], P('group', 'fsdp')
- new_first: bfloat16 [16, 2560, 2560], P('group', 'fsdp')
- new_second: bfloat16 [16, 2560, 2560], P('group', 'fsdp')
The draws below stay inside these ranges and needn't reach their ends.
Inputs may be any that keep to these rules, and one draw needn't show every extreme that they name: `token_ids`: token ids of a vocabulary of 32000, or -100 for tokens outside the loss; some token of every draw is -100 and some is 31999.
All inputs are finite; a program needn't handle non-finite values.
Results may differ from the reference program's by a relative error of at most 0.014.
Values may be sent and summed in bfloat16 or wider, within the bound.
No kernel may reach another device: no remote copies, remote signals or barrier semaphores. Data moves between devices by JAX's collectives and lax.ppermute only.
A program may use at most 128 MiB of HBM per device.

```python
import math
import jax
import jax.numpy as jnp

HD = 2560
DW = 2560
VOCAB = 32000
TOK_GROUP = 4096
GROUPS = 16
TOK_DEV = 256
TOKENS = 65536
N_GROUP = 16
N_FSDP = 16


def draw_token_ids(key, part):
    key = jax.random.fold_in(key, 7)
    key_vals, key_dropped = jax.random.split(key)
    token_vals = jax.random.randint(key_vals, (TOKENS,), 0, VOCAB)
    dropped = jax.random.randint(key_dropped, (TOKENS,), 0, 8)
    token_vals = jnp.where(dropped == 0, -100, token_vals)
    token_vals = token_vals.at[0].set(-100).at[1].set(VOCAB - 1)
    return token_vals.astype(jnp.int32)


def raised(values, key, source, target, shards_of, factor):
    owner, partner = [(jnp.arange(values.shape[axis_at]) // (values.shape[axis_at] // shards_of)).reshape([-1 if axis == axis_at else 1 for axis in range(values.ndim)]) for axis_at in (source, target)]
    chosen = jax.random.permutation(key, shards_of)[partner]
    strong = (owner == chosen) | (owner == (partner + shards_of // 2) % shards_of)
    return jnp.where(strong, factor * values, values)


def block_levels(stream_key, shape, cuts, smallest, high):
    gain, own = 1.0, jax.random.fold_in(stream_key, 6)
    for axis_at, shards_of in cuts:
        draws = jnp.exp(jax.random.uniform(jax.random.fold_in(own, axis_at), (shards_of,), jnp.float32, smallest / len(cuts), high / len(cuts)))
        gain = gain * jnp.repeat(draws, shape[axis_at] // shards_of).reshape([-1 if axis == axis_at else 1 for axis in range(len(shape))])
    return gain


def scatter_about(stream_key, dims, width, most, shards=(), held_as=jnp.bfloat16):
    drawn = jax.random.normal(stream_key, dims, jnp.float32) * width
    if len(shards) > 0:
        drawn = block_levels(stream_key, dims, shards, -0.22, 0.18) * drawn
    return jnp.clip(drawn, min=-most, max=most).astype(held_as)


def gaussian_with(rng, dims, scale, limit, pieces, heavy, kind=jnp.bfloat16):
    entries = scale * jax.random.normal(rng, dims, jnp.float32)
    if pieces:
        entries = entries * block_levels(rng, dims, pieces, -0.22, 0.18)
    return jnp.clip(raised(entries, jax.random.fold_in(rng, 3), *heavy), -limit, limit).astype(kind)


def setup_inputs(seed: int = 0) -> dict:
    arg_keys = jax.random.split(jax.random.key(seed), 8)
    activations = gaussian_with(arg_keys[0], (TOKENS, HD), 1.0, 24.0, ((0, 256),), (0, 1, 256, 6.0))
    cotangent = scatter_about(arg_keys[1], (TOKENS, DW), 1.0, 6.0, ((0, 256),))
    token_ids = draw_token_ids(jax.random.fold_in(arg_keys[7], 71), 0)
    step_count = jax.random.randint(arg_keys[3], (1,), 0, 8).astype(jnp.int32)
    master = scatter_about(arg_keys[4], (GROUPS, HD, DW), 0.02, 0.12, ((0, 16), (1, 16)), jnp.float32)
    first_moment = scatter_about(arg_keys[5], (GROUPS, HD, DW), 30.0, 150.0, ((0, 16), (1, 16)))
    second_moment = jnp.clip(jnp.exp(math.log(3200.0) - 2.7725887 * jax.random.uniform(arg_keys[6], (GROUPS, HD, DW), jnp.float32) ** block_levels(arg_keys[6], (GROUPS, HD, DW), ((0, 16), (1, 16)), -0.2, 0.2)), 200.0, 3200.0).astype(jnp.bfloat16)
    return {"activations": activations, "cotangent": cotangent, "token_ids": token_ids, "step_count": step_count, "master": master, "first_moment": first_moment, "second_moment": second_moment}


beta_one = 0.9
beta_two = 0.95
learn_rate = 0.002
decay_rate = 0.1
epsilon = 1e-05

def adam_delta(master_rows, first_rows, second_rows, gradient, step_count):
    steps_done = (step_count[0] + 1).astype(jnp.float32)
    first_new = beta_one * first_rows.astype(jnp.float32) + (1.0 - beta_one) * gradient
    second_new = beta_two * second_rows.astype(jnp.float32) + (1.0 - beta_two) * gradient * gradient
    first_hat = first_new / (1.0 - jnp.power(jnp.float32(beta_one), steps_done))
    second_hat = second_new / (1.0 - jnp.power(jnp.float32(beta_two), steps_done))
    delta = learn_rate * (first_hat / (jnp.sqrt(second_hat) + epsilon) + decay_rate * master_rows)
    return (delta, first_new.astype(jnp.bfloat16), second_new.astype(jnp.bfloat16))

def reference(activations, cotangent, token_ids, step_count, master, first_moment, second_moment):
    outputs = []
    act_grads = []
    stepped_all = []
    firsts = []
    seconds = []
    for group_index in range(GROUPS):
        lower = group_index * TOK_GROUP
        upper = lower + TOK_GROUP
        weights = master[group_index].astype(jnp.bfloat16)
        acts_group = activations[lower:upper]
        live_grad = jnp.where((token_ids[lower:upper] >= 0)[:, None], cotangent[lower:upper], jnp.zeros((), cotangent.dtype))
        outputs.append(jnp.dot(acts_group, weights, preferred_element_type=jnp.float32).astype(jnp.bfloat16))
        act_grads.append(jnp.dot(live_grad, weights.T, preferred_element_type=jnp.float32).astype(jnp.bfloat16))
        gradient = jnp.zeros((HD, DW), jnp.float32)
        for block in range(N_FSDP):
            rows_lo = block * TOK_DEV
            rows_hi = rows_lo + TOK_DEV
            partial_term = jnp.dot(acts_group[rows_lo:rows_hi].T, live_grad[rows_lo:rows_hi], preferred_element_type=jnp.float32)
            gradient = gradient + partial_term.astype(jnp.bfloat16).astype(jnp.float32)
        delta, first_out, second_out = adam_delta(master[group_index], first_moment[group_index], second_moment[group_index], gradient, step_count)
        stepped_all.append(master[group_index] - delta)
        firsts.append(first_out)
        seconds.append(second_out)
    stepped = jnp.stack(stepped_all)
    levels = N_GROUP.bit_length() - 1
    bit_index = step_count[0] % levels
    partner = jnp.bitwise_xor(jnp.arange(GROUPS, dtype=jnp.int32), jnp.left_shift(jnp.int32(1), bit_index).astype(jnp.int32))
    new_master = 0.5 * (stepped + jnp.take(stepped, partner, axis=0))
    return (jnp.concatenate(outputs, 0), jnp.concatenate(act_grads, 0), new_master, jnp.stack(firsts), jnp.stack(seconds))
```

```python
from functools import partial

import jax
import jax.numpy as jnp
from jax import lax
from jax.experimental import pallas as pl
from jax.experimental.pallas import tpu as pltpu
from jax.sharding import PartitionSpec as P

beta_one = 0.9
beta_two = 0.95
learn_rate = 0.002
decay_rate = 0.1
epsilon = 1e-05

NX = 4
PIECE = 160
HALF = NX * PIECE

bf16 = jnp.bfloat16
f32 = jnp.float32
SMEM = pl.BlockSpec(memory_space=pltpu.SMEM)
VMEM = pl.BlockSpec(memory_space=pltpu.VMEM)
ANY = pl.BlockSpec(memory_space=pl.ANY)
LIMIT = pltpu.CompilerParams(vmem_limit_bytes=48 * 1024 * 1024)


def along(move):
    pairs = []
    for f in range(16):
        x, h, c = move(f // 4, (f // 2) % 2, f % 2)
        pairs.append((f, (x % 4) * 4 + h * 2 + c))
    return pairs


NEXT = along(lambda x, h, c: (x + 1, h, c))
PREV = along(lambda x, h, c: (x - 1, h, c))
OPPOSITE = along(lambda x, h, c: (x + 2, h, c))
ACROSS = along(lambda x, h, c: (x, 1 - h, c))
DIAGONAL = along(lambda x, h, c: (x, 1 - h, 1 - c))
SIBLING = along(lambda x, h, c: (x, h, 1 - c))


def send(value, pairs):
    return lax.ppermute(value, "fsdp", pairs)


def cost(flops, moved):
    return pl.CostEstimate(flops=1, bytes_accessed=1, transcendentals=0)


def held_until(value, after):
    return pl.pallas_call(
        lambda *refs: None,
        out_shape=jax.ShapeDtypeStruct(value.shape, value.dtype),
        in_specs=[ANY] * (1 + len(after)),
        out_specs=ANY,
        input_output_aliases={0: 0},
        cost_estimate=cost(0, 0),
    )(value, *after)


def row_of(place, h, slot, j):
    x, c = place[0], place[2]
    core = c if slot == 0 else 1 - c
    return pl.multiple_of(lax.rem(x + j, NX) * (4 * PIECE) + h * (2 * PIECE) + core * PIECE, 32)


def prepare_kernel(place, act, cot, live, master, bias, masked, own, sib, other, shard, flipped, ordered):
    h = place[1]
    flipped[...] = act[...].T
    for slot in range(2):
        for j in range(NX):
            start = slot * HALF + j * PIECE
            ordered[pl.ds(start, PIECE), :] = flipped[pl.ds(row_of(place, 1 - h, slot, j), PIECE), :]
            start += 2 * HALF
            ordered[pl.ds(start, PIECE), :] = flipped[pl.ds(row_of(place, h, slot, j), PIECE), :]
    other[...] = ordered[: 2 * HALF, :].T
    own[...] = ordered[2 * HALF : 3 * HALF, :].T
    sib[...] = ordered[3 * HALF :, :].T
    masked[...] = jnp.where(live[...] >= 0, cot[...], jnp.zeros((), bf16))
    shard[...] = master[...].astype(bf16)


def prepare(place, activations, cotangent, token_ids, master, bias):
    rows, wide = activations.shape
    shapes = [(rows, wide), (rows, HALF), (rows, HALF), (rows, 2 * HALF), master.shape]
    return pl.pallas_call(
        prepare_kernel,
        out_shape=[jax.ShapeDtypeStruct(shape, bf16) for shape in shapes],
        in_specs=[SMEM, VMEM, VMEM, VMEM, VMEM, SMEM],
        out_specs=[VMEM] * 5,
        scratch_shapes=[pltpu.VMEM((wide, rows), bf16), pltpu.VMEM((wide, rows), bf16)],
        compiler_params=LIMIT,
        cost_estimate=cost(0, 8 * rows * wide),
    )(place, activations, cotangent, token_ids[:, None], master, bias)


OVER_ROWS = (((0,), (0,)), ((), ()))
OVER_COLUMNS = (((1,), (1,)), ((), ()))


def gradient_kernel(*refs):
    acts, grads, outs = refs[0:4], refs[4:8], refs[-NX:]
    wide = grads[0].shape[1]
    width = wide // 2
    for cols in (slice(0, width), slice(width, wide)):
        total = None
        for act, grad in zip(acts, grads):
            term = lax.dot_general(act[...], grad[:, cols], OVER_ROWS, preferred_element_type=f32)
            total = term if total is None else total + term
        for j in range(NX):
            outs[j][:, cols] = total[j * PIECE : (j + 1) * PIECE].astype(outs[j].dtype)


def gradient_blocks(acts, grads, after):
    rows, wide = grads[0].shape
    first = pl.BlockSpec((rows, HALF), lambda i: (0, 0))
    last = pl.BlockSpec((rows, HALF), lambda i: (0, 1))
    whole = pl.BlockSpec((rows, wide), lambda i: (0, 0))
    out = pl.BlockSpec((PIECE, wide), lambda i: (0, 0))
    return pl.pallas_call(
        gradient_kernel,
        grid=(1,),
        out_shape=[jax.ShapeDtypeStruct((PIECE, wide), f32)]
        + [jax.ShapeDtypeStruct((PIECE, wide), bf16)] * (NX - 1),
        in_specs=[first, first, first, last] + [whole] * 4 + [ANY] * len(after),
        out_specs=[out] * NX,
        compiler_params=LIMIT,
        cost_estimate=cost(8 * HALF * rows * wide, 10_000_000),
    )(*acts, *grads, *after)


def fetch(shards, gathered, sems):
    copies = []
    start = 0
    for i, shard in enumerate(shards):
        to = gathered.at[pl.ds(start, shard.shape[0]), :]
        copies.append(pltpu.make_async_copy(shard, to, sems.at[i]))
        start += shard.shape[0]
    for copy in copies:
        copy.start()
    for copy in copies:
        copy.wait()


def times_weights(flipped, gathered):
    return lax.dot_general(flipped, gathered, (((0,), (0,)), ((), ())), preferred_element_type=f32)


def output_kernel(count, own, sib, other, *refs):
    shards = refs[:count]
    theirs, ours, gathered, sems = refs[-4:]
    fetch(shards, gathered, sems)
    theirs[...] = jnp.dot(other[...], gathered[...], preferred_element_type=f32).astype(bf16)
    total = jnp.dot(own[...], gathered[:HALF, :], preferred_element_type=f32)
    ours[...] = total + jnp.dot(sib[...], gathered[HALF:, :], preferred_element_type=f32)


def output_parts(own, sib, other, weights):
    rows, depth = other.shape
    wide = weights[0].shape[1]
    return pl.pallas_call(
        partial(output_kernel, len(weights)),
        out_shape=[jax.ShapeDtypeStruct((rows, wide), bf16), jax.ShapeDtypeStruct((rows, wide), f32)],
        in_specs=[VMEM] * 3 + [ANY] * len(weights),
        out_specs=[VMEM] * 2,
        scratch_shapes=[pltpu.VMEM((depth, wide), bf16), pltpu.SemaphoreType.DMA((len(weights),))],
        compiler_params=LIMIT,
        cost_estimate=cost(4 * depth * rows * wide, 2 * depth * wide + 8 * rows * wide),
    )(own, sib, other, *weights)


def act_grad_kernel(count, masked, across, *refs):
    shards = refs[:count]
    theirs, ours, gathered, sems = refs[-4:]
    fetch(shards, gathered, sems)
    for out, grad in ((theirs, across), (ours, masked)):
        back = lax.dot_general(gathered[...], grad[...], OVER_COLUMNS, preferred_element_type=f32)
        out[...] = back.astype(bf16)


def act_grad_parts(masked, across, weights, after):
    rows, wide = masked.shape
    depth = 2 * HALF
    return pl.pallas_call(
        partial(act_grad_kernel, len(weights)),
        out_shape=[jax.ShapeDtypeStruct((depth, rows), bf16)] * 2,
        in_specs=[VMEM] * 2 + [ANY] * (len(weights) + len(after)),
        out_specs=[VMEM] * 2,
        scratch_shapes=[pltpu.VMEM((depth, wide), bf16), pltpu.SemaphoreType.DMA((len(weights),))],
        compiler_params=LIMIT,
        cost_estimate=cost(4 * depth * rows * wide, 2 * depth * wide + 6 * rows * wide),
    )(masked, across, *weights, *after)


def assemble_kernel(place, ours, theirs, *refs):
    out, flipped = refs[-2:]
    h = place[1]
    for slot in range(2):
        for j in range(NX):
            start = slot * HALF + j * PIECE
            flipped[pl.ds(row_of(place, h, slot, j), PIECE), :] = ours[start : start + PIECE, :]
            flipped[pl.ds(row_of(place, 1 - h, slot, j), PIECE), :] = theirs[start : start + PIECE, :]
    out[...] = flipped[...].T


def assemble(place, ours, theirs, after):
    depth, rows = ours.shape
    return pl.pallas_call(
        assemble_kernel,
        out_shape=jax.ShapeDtypeStruct((rows, 2 * depth), bf16),
        in_specs=[SMEM, VMEM, VMEM] + [ANY] * len(after),
        out_specs=VMEM,
        scratch_shapes=[pltpu.VMEM((2 * depth, rows), bf16)],
        compiler_params=LIMIT,
        cost_estimate=cost(0, 8 * rows * depth),
    )(place, ours, theirs, *after)


def adam_kernel(bias, master, first, second, here, *refs):
    arrived = refs[: NX - 1]
    stepped, sent, first_out, second_out = refs[-4:]
    gradient = here[...]
    for part in arrived:
        gradient += part[...].astype(f32)
    rows = master[...]
    first_new = beta_one * first[...].astype(f32) + (1.0 - beta_one) * gradient
    second_new = beta_two * second[...].astype(f32) + (1.0 - beta_two) * gradient * gradient
    first_hat = first_new / bias[0]
    second_hat = second_new / bias[1]
    delta = learn_rate * (first_hat / (jnp.sqrt(second_hat) + epsilon) + decay_rate * rows)
    stepped[...] = rows - delta
    sent[...] = (rows - delta).astype(bf16)
    first_out[...] = first_new.astype(bf16)
    second_out[...] = second_new.astype(bf16)


def adam(bias, master, first, second, parts):
    rows, wide = master.shape
    steps = 5
    part = pl.BlockSpec((rows // steps, wide), lambda i: (i, 0))
    return pl.pallas_call(
        adam_kernel,
        grid=(steps,),
        out_shape=[jax.ShapeDtypeStruct((rows, wide), f32)] + [jax.ShapeDtypeStruct((rows, wide), bf16)] * 3,
        in_specs=[SMEM] + [part] * (3 + len(parts)),
        out_specs=[part] * 4,
        compiler_params=LIMIT,
        cost_estimate=cost(20 * rows * wide, 26 * rows * wide),
    )(bias, master, first, second, *parts)


def finish_kernel(base, arrived, stepped, other, output, averaged):
    output[...] = (base[...] + arrived[...].astype(f32)).astype(bf16)
    averaged[...] = 0.5 * (stepped[...] + other[...].astype(f32))


def finish(base, arrived, stepped, other):
    rows, wide = base.shape
    mine = stepped.shape[0]
    steps = 5
    cols = pl.BlockSpec((rows, wide // steps), lambda i: (0, i))
    part = pl.BlockSpec((mine // steps, wide), lambda i: (i, 0))
    return pl.pallas_call(
        finish_kernel,
        grid=(steps,),
        out_shape=[jax.ShapeDtypeStruct((rows, wide), bf16), jax.ShapeDtypeStruct((mine, wide), f32)],
        in_specs=[cols, cols, part, part],
        out_specs=[cols, part],
        compiler_params=LIMIT,
        cost_estimate=cost(4 * rows * wide, 14 * rows * wide),
    )(base, arrived, stepped, other)


def from_partner(value, bit_index):
    mask = 2**bit_index
    pairs = [(source, source ^ mask) for source in range(lax.axis_size("group"))]
    return lax.ppermute(value, "group", pairs)


def exchange(sent, beside, bit_index):
    levels = lax.axis_size("group").bit_length() - 1

    def branch(level, value, rest):
        return from_partner(value, level), [send(part, pairs) for part, pairs in zip(rest, moves)]

    rest, moves = [part for part, _ in beside], [pairs for _, pairs in beside]
    return lax.switch(bit_index, [partial(branch, level) for level in range(levels)], sent, rest)


def shards(activations, cotangent, token_ids, step_count, master, first_moment, second_moment):
    master, first_old, second_old = master[0], first_moment[0], second_moment[0]
    levels = lax.axis_size("group").bit_length() - 1
    bit_index = step_count[0] % levels
    f = lax.axis_index("fsdp")
    place = jnp.stack([f // 4, (f // 2) % 2, f % 2]).astype(jnp.int32)
    steps_done = (step_count[0] + 1).astype(f32)
    bias = jnp.stack([1.0 - jnp.power(f32(beta_one), steps_done), 1.0 - jnp.power(f32(beta_two), steps_done)])

    masked, own, sib, other, shard = prepare(place, activations, cotangent, token_ids, master, bias)
    across_act, across = send(other, ACROSS), send(masked, ACROSS)
    pieces = [shard, send(shard, PREV), send(shard, OPPOSITE), send(shard, NEXT)]
    weights = pieces + [send(part, SIBLING) for part in pieces]
    output, base = output_parts(own, sib, across_act, weights)
    output = send(output, ACROSS)
    across = held_until(across, [base])
    acts = [own, send(sib, SIBLING), across_act, send(across_act, SIBLING)]
    grads = [masked, send(masked, SIBLING), across, send(across, SIBLING)]

    here, *away = gradient_blocks(acts, grads, [base])
    away = [send(part, pairs) for part, pairs in zip(away, (NEXT, OPPOSITE, PREV))]
    theirs, ours = act_grad_parts(masked, across, weights, [here])
    stepped, sent, first_out, second_out = adam(bias, master, first_old, second_old, [here, *away])
    arrived, (theirs,) = exchange(sent, [(theirs, ACROSS)], bit_index)
    act_grad = assemble(place, ours, theirs, [])
    output, averaged = finish(base, output, stepped, arrived)
    return (output, act_grad, averaged[None], first_out[None], second_out[None])


def solution(mesh):
    rows = P(("group", "fsdp"), None)
    state = P("group", "fsdp", None)
    return jax.shard_map(
        shards,
        mesh=mesh,
        in_specs=(rows, rows, P(("group", "fsdp")), P(), state, state, state),
        out_specs=(rows, rows, state, state, state),
        check_vma=False,
    )
```

```python
from functools import partial

import jax
import jax.numpy as jnp
from jax import lax
from jax.experimental import pallas as pl
from jax.experimental.pallas import tpu as pltpu
from jax.sharding import PartitionSpec as P

beta_one = 0.9
beta_two = 0.95
learn_rate = 0.002
decay_rate = 0.1
epsilon = 1e-05

NX = 4
PIECE = 160
HALF = NX * PIECE

bf16 = jnp.bfloat16
f32 = jnp.float32
SMEM = pl.BlockSpec(memory_space=pltpu.SMEM)
VMEM = pl.BlockSpec(memory_space=pltpu.VMEM)
ANY = pl.BlockSpec(memory_space=pltpu.HBM)


def room(mebibytes):
    return pltpu.CompilerParams(vmem_limit_bytes=mebibytes * 1024 * 1024)


def along(move):
    pairs = []
    for f in range(16):
        x, h, c = move(f // 4, (f // 2) % 2, f % 2)
        pairs.append((f, (x % 4) * 4 + h * 2 + c))
    return pairs


NEXT = along(lambda x, h, c: (x + 1, h, c))
PREV = along(lambda x, h, c: (x - 1, h, c))
OPPOSITE = along(lambda x, h, c: (x + 2, h, c))
ACROSS = along(lambda x, h, c: (x, 1 - h, c))
DIAGONAL = along(lambda x, h, c: (x, 1 - h, 1 - c))
SIBLING = along(lambda x, h, c: (x, h, 1 - c))


def send(value, pairs):
    return lax.ppermute(value, "fsdp", pairs)


def cost(flops, moved):
    return pl.CostEstimate(flops=1, bytes_accessed=1, transcendentals=0)


def held_until(value, after):
    return pl.pallas_call(
        lambda *refs: None,
        out_shape=jax.ShapeDtypeStruct(value.shape, value.dtype),
        in_specs=[ANY] * (1 + len(after)),
        out_specs=ANY,
        input_output_aliases={0: 0},
        compiler_params=room(1),
        cost_estimate=cost(0, 0),
    )(value, *after)


def row_of(place, h, slot, j):
    x, c = place[0], place[2]
    core = c if slot == 0 else 1 - c
    return pl.multiple_of(lax.rem(x + j, NX) * (4 * PIECE) + h * (2 * PIECE) + core * PIECE, 32)


def prepare_kernel(place, act, cot, live, master, bias, mine, lead, own, shard, flipped, ordered):
    h = place[1]
    flipped[...] = act[...].T
    for slot in range(2):
        for j in range(NX):
            start = slot * HALF + j * PIECE
            ordered[pl.ds(start, PIECE), :] = flipped[pl.ds(row_of(place, 1 - h, slot, j), PIECE), :]
            start += 2 * HALF
            ordered[pl.ds(start, PIECE), :] = flipped[pl.ds(row_of(place, h, slot, j), PIECE), :]
    wide = cot.shape[1]
    lead[:, wide:] = ordered[: 2 * HALF, :].T
    own[...] = ordered[2 * HALF : 3 * HALF, :].T
    mine[:, wide:] = ordered[3 * HALF :, :].T
    masked = jnp.where(live[...] >= 0, cot[...], jnp.zeros((), bf16))
    lead[:, :wide] = masked
    mine[:, :wide] = masked
    shard[...] = master[...].astype(bf16)


def prepare(place, activations, cotangent, token_ids, master, bias):
    rows, wide = activations.shape
    shapes = [(rows, wide + HALF), (rows, wide + 2 * HALF), (rows, HALF), master.shape]
    return pl.pallas_call(
        prepare_kernel,
        out_shape=[jax.ShapeDtypeStruct(shape, bf16) for shape in shapes],
        in_specs=[SMEM, VMEM, VMEM, VMEM, VMEM, SMEM],
        out_specs=[VMEM] * 4,
        scratch_shapes=[pltpu.VMEM((wide, rows), bf16), pltpu.VMEM((wide, rows), bf16)],
        compiler_params=room(14),
        cost_estimate=cost(0, 8 * rows * wide),
    )(place, activations, cotangent, token_ids[:, None], master, bias)


OVER_ROWS = (((0,), (0,)), ((), ()))
OVER_COLUMNS = (((1,), (1,)), ((), ()))


def gradient_kernel(*refs):
    acts, grads, outs, flipped, gathered = refs[0:4], refs[4:8], refs[-2 * NX - 1 : -2], refs[-2], refs[-1]
    rows = grads[0].shape[0]

    @pl.when(pl.program_id(0) == 0)
    def _():
        for i, act in enumerate(acts):
            flipped[:, i * rows : (i + 1) * rows] = act[...].T

    for i, grad in enumerate(grads):
        gathered[i * rows : (i + 1) * rows, :] = grad[...]
    total = jnp.dot(flipped[...], gathered[...], preferred_element_type=f32)
    start = 0
    for out in outs:
        out[...] = total[start : start + out.shape[0]].astype(out.dtype)
        start += out.shape[0]


def gradient_blocks(own, mine, beside, lead, diagonal, after):
    rows = own.shape[0]
    wide = mine.shape[1] - HALF
    steps = 5
    whole = pl.BlockSpec((rows, HALF), lambda i: (0, 0))
    first = pl.BlockSpec((rows, HALF), lambda i: (0, wide // HALF))
    last = pl.BlockSpec((rows, HALF), lambda i: (0, wide // HALF + 1))
    cols = pl.BlockSpec((rows, wide // steps), lambda i: (0, i))
    out = pl.BlockSpec((PIECE, wide // steps), lambda i: (0, i))
    half = pl.BlockSpec((PIECE // 2, wide // steps), lambda i: (0, i))
    return pl.pallas_call(
        gradient_kernel,
        grid=(steps,),
        out_shape=[jax.ShapeDtypeStruct((PIECE, wide), f32)]
        + [jax.ShapeDtypeStruct((PIECE // 2, wide), bf16)] * (2 * NX - 2),
        in_specs=[whole, first, first, last] + [cols] * 4 + [ANY] * len(after),
        out_specs=[out] + [half] * (2 * NX - 2),
        scratch_shapes=[pltpu.VMEM((HALF, 4 * rows), bf16), pltpu.VMEM((4 * rows, wide // steps), bf16)],
        compiler_params=room(16),
        cost_estimate=cost(8 * HALF * rows * wide, 10_000_000),
    )(own, beside, lead, diagonal, mine, beside, lead, diagonal, *after)


def join_kernel(*refs):
    for left, right, out in zip(refs[0:2], refs[2:4], refs[4:6]):
        out[...] = (left[...].astype(f32) + right[...].astype(f32)).astype(bf16)


def join(ours, arrived):
    shape = ours[0].shape
    return pl.pallas_call(
        join_kernel,
        out_shape=[jax.ShapeDtypeStruct(shape, bf16)] * 2,
        in_specs=[VMEM] * 4,
        out_specs=[VMEM] * 2,
        compiler_params=room(6),
        cost_estimate=cost(2 * shape[0] * shape[1], 12 * shape[0] * shape[1]),
    )(*ours, *arrived)


def fetch(shards, gathered, sems):
    copies = []
    start = 0
    for i, shard in enumerate(shards):
        to = gathered.at[pl.ds(start, shard.shape[0]), :]
        copies.append(pltpu.make_async_copy(shard, to, sems.at[i]))
        start += shard.shape[0]
    for copy in copies:
        copy.start()
    for copy in copies:
        copy.wait()


def times_weights(flipped, gathered):
    return lax.dot_general(flipped, gathered, (((0,), (0,)), ((), ())), preferred_element_type=f32)


def output_kernel(count, lead, *refs):
    shards, (theirs, gathered) = refs[:count], refs[-2:]
    for i, shard in enumerate(shards):
        gathered[i * PIECE : (i + 1) * PIECE, :] = shard[...]
    theirs[...] = jnp.dot(lead[...], gathered[...], preferred_element_type=f32).astype(bf16)


def output_part(lead, weights, after):
    depth = 2 * HALF
    rows = lead.shape[0]
    wide = weights[0].shape[1]
    steps = 5
    tile = wide // steps
    return pl.pallas_call(
        partial(output_kernel, len(weights)),
        grid=(steps,),
        out_shape=jax.ShapeDtypeStruct((rows, wide), bf16),
        in_specs=[pl.BlockSpec((rows, depth), lambda i: (0, wide // depth))]
        + [pl.BlockSpec((PIECE, tile), lambda i: (0, i))] * len(weights)
        + [ANY] * len(after),
        out_specs=pl.BlockSpec((rows, tile), lambda i: (0, i)),
        scratch_shapes=[pltpu.VMEM((depth, tile), bf16)],
        compiler_params=room(12),
        cost_estimate=cost(2 * depth * rows * wide, 2 * depth * wide + 4 * rows * wide),
    )(lead, *weights, *after)


def products_kernel(count, mine, lead, own, *refs):
    shards = refs[:count]
    theirs, ours, base, gathered, sems = refs[-5:]
    fetch(shards, gathered, sems)
    wide = base.shape[1]
    for out, grad in ((theirs, lead), (ours, mine)):
        back = lax.dot_general(gathered[...], grad[:, :wide], OVER_COLUMNS, preferred_element_type=f32)
        out[...] = back.astype(bf16)
    total = jnp.dot(own[...], gathered[:HALF, :], preferred_element_type=f32)
    base[...] = total + jnp.dot(mine[:, wide:], gathered[HALF:, :], preferred_element_type=f32)


def products(mine, lead, own, weights, after):
    depth = 2 * HALF
    rows = own.shape[0]
    wide = weights[0].shape[1]
    return pl.pallas_call(
        partial(products_kernel, len(weights)),
        out_shape=[jax.ShapeDtypeStruct((depth, rows), bf16)] * 2 + [jax.ShapeDtypeStruct((rows, wide), f32)],
        in_specs=[VMEM] * 3 + [ANY] * (len(weights) + len(after)),
        out_specs=[VMEM] * 3,
        scratch_shapes=[pltpu.VMEM((depth, wide), bf16), pltpu.SemaphoreType.DMA((len(weights),))],
        compiler_params=room(22),
        cost_estimate=cost(6 * depth * rows * wide, 2 * depth * wide + 10 * rows * wide),
    )(mine, lead, own, *weights, *after)


def adam_kernel(bias, master, first, second, here, *refs):
    low, high = refs[0:2], refs[2:4]
    stepped, sent, first_out, second_out = refs[-4:]

    def update(arrived):
        gradient = here[...]
        for part in arrived:
            gradient += part[...].astype(f32)
        rows = master[...]
        first_new = beta_one * first[...].astype(f32) + (1.0 - beta_one) * gradient
        second_new = beta_two * second[...].astype(f32) + (1.0 - beta_two) * gradient * gradient
        first_hat = first_new / bias[0]
        second_hat = second_new / bias[1]
        delta = learn_rate * (first_hat / (jnp.sqrt(second_hat) + epsilon) + decay_rate * rows)
        stepped[...] = rows - delta
        sent[...] = (rows - delta).astype(bf16)
        first_out[...] = first_new.astype(bf16)
        second_out[...] = second_new.astype(bf16)

    first_half = pl.program_id(0) < pl.num_programs(0) // 2

    @pl.when(first_half)
    def _():
        update(low)

    @pl.when(jnp.logical_not(first_half))
    def _():
        update(high)


def adam(bias, master, first, second, here, low, high):
    rows, wide = master.shape
    steps = 2
    turn = steps // 2
    part = pl.BlockSpec((rows // steps, wide), lambda i: (i, 0))
    lows = pl.BlockSpec((rows // steps, wide), lambda i: (jnp.minimum(i, turn - 1), 0))
    highs = pl.BlockSpec((rows // steps, wide), lambda i: (jnp.maximum(i - turn, 0), 0))
    return pl.pallas_call(
        adam_kernel,
        grid=(steps,),
        out_shape=[jax.ShapeDtypeStruct((rows, wide), f32)] + [jax.ShapeDtypeStruct((rows, wide), bf16)] * 3,
        in_specs=[SMEM] + [part] * 4 + [lows] * 2 + [highs] * 2,
        out_specs=[part] * 4,
        compiler_params=room(18),
        cost_estimate=cost(20 * rows * wide, 26 * rows * wide),
    )(bias, master, first, second, here, *low, *high)


def finish_kernel(place, ours, theirs, base, arrived, stepped, other, output, act_grad, averaged, ordered):
    h = place[1]
    step = pl.program_id(0)

    @pl.when(step == 0)
    def _():
        for slot in range(2):
            for j in range(NX):
                start = slot * HALF + j * PIECE
                piece = slice(start, start + PIECE)
                ordered[pl.ds(row_of(place, h, slot, j), PIECE), :] = ours[piece, :]
                ordered[pl.ds(row_of(place, 1 - h, slot, j), PIECE), :] = theirs[piece, :]

    width = act_grad.shape[1]
    act_grad[...] = ordered[pl.ds(pl.multiple_of(step * width, width), width), :].T
    output[...] = (base[...] + arrived[...].astype(f32)).astype(bf16)
    averaged[...] = 0.5 * (stepped[...] + other[...].astype(f32))


def finish(place, ours, theirs, base, arrived, stepped, other):
    rows, wide = base.shape
    depth = ours.shape[0]
    mine = stepped.shape[0]
    steps = 5
    cols = pl.BlockSpec((rows, wide // steps), lambda i: (0, i))
    part = pl.BlockSpec((mine // steps, wide), lambda i: (i, 0))
    whole = pl.BlockSpec((depth, rows), lambda i: (0, 0))
    return pl.pallas_call(
        finish_kernel,
        grid=(steps,),
        out_shape=[
            jax.ShapeDtypeStruct((rows, wide), bf16),
            jax.ShapeDtypeStruct((rows, 2 * depth), bf16),
            jax.ShapeDtypeStruct((mine, wide), f32),
        ],
        in_specs=[SMEM, whole, whole, cols, cols, part, part],
        out_specs=[cols, cols, part],
        scratch_shapes=[pltpu.VMEM((2 * depth, rows), bf16)],
        compiler_params=room(14),
        cost_estimate=cost(4 * rows * wide, 18 * rows * wide),
    )(place, ours, theirs, base, arrived, stepped, other)


def from_partner(value, bit_index):
    mask = 2**bit_index
    pairs = [(source, source ^ mask) for source in range(lax.axis_size("group"))]
    return lax.ppermute(value, "group", pairs)


def exchange(sent, beside, bit_index):
    levels = lax.axis_size("group").bit_length() - 1

    def branch(level, value, rest):
        return from_partner(value, level), [send(part, pairs) for part, pairs in zip(rest, moves)]

    rest, moves = [part for part, _ in beside], [pairs for _, pairs in beside]
    return lax.switch(bit_index, [partial(branch, level) for level in range(levels)], sent, rest)


def shards(activations, cotangent, token_ids, step_count, master, first_moment, second_moment):
    master, first_old, second_old = master[0], first_moment[0], second_moment[0]
    levels = lax.axis_size("group").bit_length() - 1
    bit_index = step_count[0] % levels
    f = lax.axis_index("fsdp")
    place = jnp.stack([f // 4, (f // 2) % 2, f % 2]).astype(jnp.int32)
    steps_done = (step_count[0] + 1).astype(f32)
    bias = jnp.stack([1.0 - jnp.power(f32(beta_one), steps_done), 1.0 - jnp.power(f32(beta_two), steps_done)])

    mine, lead, own, shard = prepare(place, activations, cotangent, token_ids, master, bias)
    lead, beside = send(lead, ACROSS), send(mine, SIBLING)
    pieces = [shard, send(shard, PREV), send(shard, OPPOSITE), send(shard, NEXT)]
    weights = pieces + [send(part, SIBLING) for part in pieces]
    lead = held_until(lead, [*weights[NX:], beside])
    output = output_part(lead, weights, [])
    blocks = gradient_blocks(own, mine, beside, lead, send(lead, SIBLING), [output])
    output = send(output, ACROSS)
    here, next_low, next_high, far_low, far_high, prev_low, prev_high = blocks
    next_low, prev_high = join((next_low, prev_high), (send(far_low, NEXT), send(far_high, PREV)))
    low = [send(next_low, NEXT), send(prev_low, PREV)]
    high = [send(next_high, NEXT), send(prev_high, PREV)]
    theirs, ours, base = products(mine, lead, own, weights, [next_low])
    stepped, sent, first_out, second_out = adam(bias, master, first_old, second_old, here, low, high)
    arrived, (theirs,) = exchange(sent, [(theirs, ACROSS)], bit_index)
    output, act_grad, averaged = finish(place, ours, theirs, base, output, stepped, arrived)
    return (output, act_grad, averaged[None], first_out[None], second_out[None])


def solution(mesh):
    rows = P(("group", "fsdp"), None)
    state = P("group", "fsdp", None)
    return jax.shard_map(
        shards,
        mesh=mesh,
        in_specs=(rows, rows, P(("group", "fsdp")), P(), state, state, state),
        out_specs=(rows, rows, state, state, state),
        check_vma=False,
    )
```

```python
from functools import partial

import jax
import jax.numpy as jnp
from jax import lax
from jax.experimental import pallas as pl
from jax.experimental.pallas import tpu as pltpu
from jax.sharding import PartitionSpec as P

beta_one = 0.9
beta_two = 0.95
learn_rate = 0.002
decay_rate = 0.1
epsilon = 1e-05

NX = 4
PIECE = 160
HALF = NX * PIECE

bf16 = jnp.bfloat16
f32 = jnp.float32
SMEM = pl.BlockSpec(memory_space=pltpu.SMEM)
VMEM = pl.BlockSpec(memory_space=pltpu.VMEM)
ANY = pl.BlockSpec(memory_space=pltpu.HBM)


def room(mebibytes):
    return pltpu.CompilerParams(vmem_limit_bytes=mebibytes * 1024 * 1024)


def along(move):
    pairs = []
    for f in range(16):
        x, h, c = move(f // 4, (f // 2) % 2, f % 2)
        pairs.append((f, (x % 4) * 4 + h * 2 + c))
    return pairs


NEXT = along(lambda x, h, c: (x + 1, h, c))
PREV = along(lambda x, h, c: (x - 1, h, c))
OPPOSITE = along(lambda x, h, c: (x + 2, h, c))
ACROSS = along(lambda x, h, c: (x, 1 - h, c))
DIAGONAL = along(lambda x, h, c: (x, 1 - h, 1 - c))
SIBLING = along(lambda x, h, c: (x, h, 1 - c))


def send(value, pairs):
    return lax.ppermute(value, "fsdp", pairs)


def cost(flops, moved):
    return pl.CostEstimate(flops=1, bytes_accessed=1, transcendentals=0)


def held_until(value, after):
    return pl.pallas_call(
        lambda *refs: None,
        out_shape=jax.ShapeDtypeStruct(value.shape, value.dtype),
        in_specs=[ANY] * (1 + len(after)),
        out_specs=ANY,
        input_output_aliases={0: 0},
        compiler_params=room(1),
        cost_estimate=cost(0, 0),
    )(value, *after)


def row_of(place, h, slot, j):
    x, c = place[0], place[2]
    core = c if slot == 0 else 1 - c
    return pl.multiple_of(lax.rem(x + j, NX) * (4 * PIECE) + h * (2 * PIECE) + core * PIECE, 32)


def prepare_kernel(place, act, cot, live, master, bias, mine, lead, own, shard, flipped, ordered):
    h = place[1]
    flipped[...] = act[...].T
    for slot in range(2):
        for j in range(NX):
            start = slot * HALF + j * PIECE
            ordered[pl.ds(start, PIECE), :] = flipped[pl.ds(row_of(place, 1 - h, slot, j), PIECE), :]
            start += 2 * HALF
            ordered[pl.ds(start, PIECE), :] = flipped[pl.ds(row_of(place, h, slot, j), PIECE), :]
    wide = cot.shape[1]
    lead[:, wide:] = ordered[: 2 * HALF, :].T
    own[...] = ordered[2 * HALF : 3 * HALF, :].T
    mine[:, wide:] = ordered[3 * HALF :, :].T
    masked = jnp.where(live[...] >= 0, cot[...], jnp.zeros((), bf16))
    lead[:, :wide] = masked
    mine[:, :wide] = masked
    shard[...] = master[...].astype(bf16)


def prepare(place, activations, cotangent, token_ids, master, bias):
    rows, wide = activations.shape
    shapes = [(rows, wide + HALF), (rows, wide + 2 * HALF), (rows, HALF), master.shape]
    return pl.pallas_call(
        prepare_kernel,
        out_shape=[jax.ShapeDtypeStruct(shape, bf16) for shape in shapes],
        in_specs=[SMEM, VMEM, VMEM, VMEM, VMEM, SMEM],
        out_specs=[VMEM] * 4,
        scratch_shapes=[pltpu.VMEM((wide, rows), bf16), pltpu.VMEM((wide, rows), bf16)],
        compiler_params=room(14),
        cost_estimate=cost(0, 8 * rows * wide),
    )(place, activations, cotangent, token_ids[:, None], master, bias)


OVER_ROWS = (((0,), (0,)), ((), ()))
OVER_COLUMNS = (((1,), (1,)), ((), ()))


def gradient_kernel(own, mine, beside, lead, diagonal, *refs):
    outs, flipped, gathered = refs[-2 * NX - 1 : -2], refs[-2], refs[-1]
    rows, wide = own.shape[0], outs[0].shape[1]
    acts = (own[...], beside[:, wide:], lead[:, wide : wide + HALF], diagonal[:, wide + HALF :])
    for i, act in enumerate(acts):
        flipped[:, i * rows : (i + 1) * rows] = act.T
    tile = gathered.shape[1]
    for k in range(wide // tile):
        cols = slice(k * tile, (k + 1) * tile)
        for i, grad in enumerate((mine, beside, lead, diagonal)):
            gathered[i * rows : (i + 1) * rows, :] = grad[:, cols]
        total = jnp.dot(flipped[...], gathered[...], preferred_element_type=f32)
        start = 0
        for out in outs:
            out[:, cols] = total[start : start + out.shape[0]].astype(out.dtype)
            start += out.shape[0]


def gradient_blocks(own, mine, beside, lead, diagonal, after):
    rows = own.shape[0]
    wide = mine.shape[1] - HALF
    return pl.pallas_call(
        gradient_kernel,
        out_shape=[jax.ShapeDtypeStruct((PIECE, wide), f32)]
        + [jax.ShapeDtypeStruct((PIECE // 2, wide), bf16)] * (2 * NX - 2),
        in_specs=[VMEM] * 5 + [ANY] * len(after),
        out_specs=[VMEM] * (2 * NX - 1),
        scratch_shapes=[pltpu.VMEM((HALF, 4 * rows), bf16), pltpu.VMEM((4 * rows, wide // 5), bf16)],
        compiler_params=room(10),
        cost_estimate=cost(8 * HALF * rows * wide, 10_000_000),
    )(own, mine, beside, lead, diagonal, *after)


def join_kernel(*refs):
    for left, right, out in zip(refs[0:2], refs[2:4], refs[4:6]):
        out[...] = (left[...].astype(f32) + right[...].astype(f32)).astype(bf16)


def join(ours, arrived):
    shape = ours[0].shape
    return pl.pallas_call(
        join_kernel,
        out_shape=[jax.ShapeDtypeStruct(shape, bf16)] * 2,
        in_specs=[VMEM] * 4,
        out_specs=[VMEM] * 2,
        compiler_params=room(6),
        cost_estimate=cost(2 * shape[0] * shape[1], 12 * shape[0] * shape[1]),
    )(*ours, *arrived)


def fetch(shards, gathered, sems):
    copies = []
    start = 0
    for i, shard in enumerate(shards):
        to = gathered.at[pl.ds(start, shard.shape[0]), :]
        copies.append(pltpu.make_async_copy(shard, to, sems.at[i]))
        start += shard.shape[0]
    for copy in copies:
        copy.start()
    for copy in copies:
        copy.wait()


def times_weights(flipped, gathered):
    return lax.dot_general(flipped, gathered, (((0,), (0,)), ((), ())), preferred_element_type=f32)


def output_kernel(count, lead, *refs):
    shards, (theirs, gathered) = refs[:count], refs[-2:]
    for i, shard in enumerate(shards):
        gathered[i * PIECE : (i + 1) * PIECE, :] = shard[...]
    theirs[...] = jnp.dot(lead[...], gathered[...], preferred_element_type=f32).astype(bf16)


def output_part(lead, weights, after):
    depth = 2 * HALF
    rows = lead.shape[0]
    wide = weights[0].shape[1]
    steps = 5
    tile = wide // steps
    return pl.pallas_call(
        partial(output_kernel, len(weights)),
        grid=(steps,),
        out_shape=jax.ShapeDtypeStruct((rows, wide), bf16),
        in_specs=[pl.BlockSpec((rows, depth), lambda i: (0, wide // depth))]
        + [pl.BlockSpec((PIECE, tile), lambda i: (0, i))] * len(weights)
        + [ANY] * len(after),
        out_specs=pl.BlockSpec((rows, tile), lambda i: (0, i)),
        scratch_shapes=[pltpu.VMEM((depth, tile), bf16)],
        compiler_params=room(12),
        cost_estimate=cost(2 * depth * rows * wide, 2 * depth * wide + 4 * rows * wide),
    )(lead, *weights, *after)


def products_kernel(count, mine, lead, own, *refs):
    shards = refs[:count]
    theirs, ours, base, gathered, sems = refs[-5:]
    fetch(shards, gathered, sems)
    wide = base.shape[1]
    for out, grad in ((theirs, lead), (ours, mine)):
        back = lax.dot_general(gathered[...], grad[:, :wide], OVER_COLUMNS, preferred_element_type=f32)
        out[...] = back.astype(bf16)
    total = jnp.dot(own[...], gathered[:HALF, :], preferred_element_type=f32)
    base[...] = total + jnp.dot(mine[:, wide:], gathered[HALF:, :], preferred_element_type=f32)


def products(mine, lead, own, weights, after):
    depth = 2 * HALF
    rows = own.shape[0]
    wide = weights[0].shape[1]
    return pl.pallas_call(
        partial(products_kernel, len(weights)),
        out_shape=[jax.ShapeDtypeStruct((depth, rows), bf16)] * 2 + [jax.ShapeDtypeStruct((rows, wide), f32)],
        in_specs=[VMEM] * 3 + [ANY] * (len(weights) + len(after)),
        out_specs=[VMEM] * 3,
        scratch_shapes=[pltpu.VMEM((depth, wide), bf16), pltpu.SemaphoreType.DMA((len(weights),))],
        compiler_params=room(16),
        cost_estimate=cost(6 * depth * rows * wide, 2 * depth * wide + 10 * rows * wide),
    )(mine, lead, own, *weights, *after)


def adam_kernel(bias, master, first, second, here, *refs):
    low, high = refs[0:2], refs[2:4]
    stepped, sent, first_out, second_out = refs[-4:]

    def update(arrived):
        gradient = here[...]
        for part in arrived:
            gradient += part[...].astype(f32)
        rows = master[...]
        first_new = beta_one * first[...].astype(f32) + (1.0 - beta_one) * gradient
        second_new = beta_two * second[...].astype(f32) + (1.0 - beta_two) * gradient * gradient
        first_hat = first_new / bias[0]
        second_hat = second_new / bias[1]
        delta = learn_rate * (first_hat / (jnp.sqrt(second_hat) + epsilon) + decay_rate * rows)
        stepped[...] = rows - delta
        sent[...] = (rows - delta).astype(bf16)
        first_out[...] = first_new.astype(bf16)
        second_out[...] = second_new.astype(bf16)

    first_half = pl.program_id(0) < pl.num_programs(0) // 2

    @pl.when(first_half)
    def _():
        update(low)

    @pl.when(jnp.logical_not(first_half))
    def _():
        update(high)


def adam(bias, master, first, second, here, low, high):
    rows, wide = master.shape
    steps = 2
    turn = steps // 2
    part = pl.BlockSpec((rows // steps, wide), lambda i: (i, 0))
    lows = pl.BlockSpec((rows // steps, wide), lambda i: (jnp.minimum(i, turn - 1), 0))
    highs = pl.BlockSpec((rows // steps, wide), lambda i: (jnp.maximum(i - turn, 0), 0))
    return pl.pallas_call(
        adam_kernel,
        grid=(steps,),
        out_shape=[jax.ShapeDtypeStruct((rows, wide), f32)] + [jax.ShapeDtypeStruct((rows, wide), bf16)] * 3,
        in_specs=[SMEM] + [part] * 4 + [lows] * 2 + [highs] * 2,
        out_specs=[part] * 4,
        compiler_params=room(18),
        cost_estimate=cost(20 * rows * wide, 26 * rows * wide),
    )(bias, master, first, second, here, *low, *high)


def finish_kernel(place, ours, theirs, base, arrived, stepped, other, output, act_grad, averaged, ordered):
    h = place[1]
    step = pl.program_id(0)

    @pl.when(step == 0)
    def _():
        for slot in range(2):
            for j in range(NX):
                start = slot * HALF + j * PIECE
                piece = slice(start, start + PIECE)
                ordered[pl.ds(row_of(place, h, slot, j), PIECE), :] = ours[piece, :]
                ordered[pl.ds(row_of(place, 1 - h, slot, j), PIECE), :] = theirs[piece, :]

    width = act_grad.shape[1]
    act_grad[...] = ordered[pl.ds(pl.multiple_of(step * width, width), width), :].T
    output[...] = (base[...] + arrived[...].astype(f32)).astype(bf16)
    averaged[...] = 0.5 * (stepped[...] + other[...].astype(f32))


def finish(place, ours, theirs, base, arrived, stepped, other):
    rows, wide = base.shape
    depth = ours.shape[0]
    mine = stepped.shape[0]
    steps = 5
    cols = pl.BlockSpec((rows, wide // steps), lambda i: (0, i))
    part = pl.BlockSpec((mine // steps, wide), lambda i: (i, 0))
    whole = pl.BlockSpec((depth, rows), lambda i: (0, 0))
    return pl.pallas_call(
        finish_kernel,
        grid=(steps,),
        out_shape=[
            jax.ShapeDtypeStruct((rows, wide), bf16),
            jax.ShapeDtypeStruct((rows, 2 * depth), bf16),
            jax.ShapeDtypeStruct((mine, wide), f32),
        ],
        in_specs=[SMEM, whole, whole, cols, cols, part, part],
        out_specs=[cols, cols, part],
        scratch_shapes=[pltpu.VMEM((2 * depth, rows), bf16)],
        compiler_params=room(14),
        cost_estimate=cost(4 * rows * wide, 18 * rows * wide),
    )(place, ours, theirs, base, arrived, stepped, other)


def from_partner(value, bit_index):
    mask = 2**bit_index
    pairs = [(source, source ^ mask) for source in range(lax.axis_size("group"))]
    return lax.ppermute(value, "group", pairs)


def exchange(sent, beside, bit_index):
    levels = lax.axis_size("group").bit_length() - 1

    def branch(level, value, rest):
        return from_partner(value, level), [send(part, pairs) for part, pairs in zip(rest, moves)]

    rest, moves = [part for part, _ in beside], [pairs for _, pairs in beside]
    return lax.switch(bit_index, [partial(branch, level) for level in range(levels)], sent, rest)


def shards(activations, cotangent, token_ids, step_count, master, first_moment, second_moment):
    master, first_old, second_old = master[0], first_moment[0], second_moment[0]
    levels = lax.axis_size("group").bit_length() - 1
    bit_index = step_count[0] % levels
    f = lax.axis_index("fsdp")
    place = jnp.stack([f // 4, (f // 2) % 2, f % 2]).astype(jnp.int32)
    steps_done = (step_count[0] + 1).astype(f32)
    bias = jnp.stack([1.0 - jnp.power(f32(beta_one), steps_done), 1.0 - jnp.power(f32(beta_two), steps_done)])

    mine, lead, own, shard = prepare(place, activations, cotangent, token_ids, master, bias)
    lead, beside = send(lead, ACROSS), send(mine, SIBLING)
    pieces = [shard, send(shard, PREV), send(shard, OPPOSITE), send(shard, NEXT)]
    weights = pieces + [send(part, SIBLING) for part in pieces]
    lead = held_until(lead, [*weights[NX:], beside])
    output = output_part(lead, weights, [])
    blocks = gradient_blocks(own, mine, beside, lead, send(lead, SIBLING), [output])
    output = send(output, ACROSS)
    here, next_low, next_high, far_low, far_high, prev_low, prev_high = blocks
    next_low, prev_high = join((next_low, prev_high), (send(far_low, NEXT), send(far_high, PREV)))
    low = [send(next_low, NEXT), send(prev_low, PREV)]
    high = [send(next_high, NEXT), send(prev_high, PREV)]
    theirs, ours, base = products(mine, lead, own, weights, [next_low])
    stepped, sent, first_out, second_out = adam(bias, master, first_old, second_old, here, low, high)
    arrived, (theirs,) = exchange(sent, [(theirs, ACROSS)], bit_index)
    output, act_grad, averaged = finish(place, ours, theirs, base, output, stepped, arrived)
    return (output, act_grad, averaged[None], first_out[None], second_out[None])


def solution(mesh):
    rows = P(("group", "fsdp"), None)
    state = P("group", "fsdp", None)
    return jax.shard_map(
        shards,
        mesh=mesh,
        in_specs=(rows, rows, P(("group", "fsdp")), P(), state, state, state),
        out_specs=(rows, rows, state, state, state),
        check_vma=False,
    )
```

```python
from functools import partial

import jax
import jax.numpy as jnp
from jax import lax
from jax.experimental import pallas as pl
from jax.experimental.pallas import tpu as pltpu
from jax.sharding import PartitionSpec as P

beta_one = 0.9
beta_two = 0.95
learn_rate = 0.002
decay_rate = 0.1
epsilon = 1e-05

NX = 4
PIECE = 160
HALF = NX * PIECE

bf16 = jnp.bfloat16
f32 = jnp.float32
SMEM = pl.BlockSpec(memory_space=pltpu.SMEM)
VMEM = pl.BlockSpec(memory_space=pltpu.VMEM)
ANY = pl.BlockSpec(memory_space=pltpu.HBM)


def room(mebibytes):
    return pltpu.CompilerParams(vmem_limit_bytes=mebibytes * 1024 * 1024)


def along(move):
    pairs = []
    for f in range(16):
        x, h, c = move(f // 4, (f // 2) % 2, f % 2)
        pairs.append((f, (x % 4) * 4 + h * 2 + c))
    return pairs


NEXT = along(lambda x, h, c: (x + 1, h, c))
PREV = along(lambda x, h, c: (x - 1, h, c))
OPPOSITE = along(lambda x, h, c: (x + 2, h, c))
ACROSS = along(lambda x, h, c: (x, 1 - h, c))
DIAGONAL = along(lambda x, h, c: (x, 1 - h, 1 - c))
SIBLING = along(lambda x, h, c: (x, h, 1 - c))


def send(value, pairs):
    return lax.ppermute(value, "fsdp", pairs)


def cost(flops, moved):
    return pl.CostEstimate(flops=1, bytes_accessed=1, transcendentals=0)


def held_until(value, after):
    return pl.pallas_call(
        lambda *refs: None,
        out_shape=jax.ShapeDtypeStruct(value.shape, value.dtype),
        in_specs=[ANY] * (1 + len(after)),
        out_specs=ANY,
        input_output_aliases={0: 0},
        compiler_params=room(1),
        cost_estimate=cost(0, 0),
    )(value, *after)


def in_hbm(value):
    return pltpu.with_memory_space_constraint(value, pltpu.HBM)


def row_of(place, h, slot, j):
    x, c = place[0], place[2]
    core = c if slot == 0 else 1 - c
    return pl.multiple_of(lax.rem(x + j, NX) * (4 * PIECE) + h * (2 * PIECE) + core * PIECE, 32)


def prepare_kernel(place, act, cot, live, master, bias, mine, lead, own, shard, act_here, cot_here, flipped, ordered, sems):
    loads = [pltpu.make_async_copy(act, act_here, sems.at[0]), pltpu.make_async_copy(cot, cot_here, sems.at[1])]
    for load in loads:
        load.start()
    loads[0].wait()
    h = place[1]
    flipped[...] = act_here[...].T
    for slot in range(2):
        for j in range(NX):
            start = slot * HALF + j * PIECE
            ordered[pl.ds(start, PIECE), :] = flipped[pl.ds(row_of(place, 1 - h, slot, j), PIECE), :]
            start += 2 * HALF
            ordered[pl.ds(start, PIECE), :] = flipped[pl.ds(row_of(place, h, slot, j), PIECE), :]
    wide = cot_here.shape[1]
    lead[:, wide:] = ordered[: 2 * HALF, :].T
    own[...] = ordered[2 * HALF : 3 * HALF, :].T
    mine[:, wide:] = ordered[3 * HALF :, :].T
    loads[1].wait()
    masked = jnp.where(live[...] >= 0, cot_here[...], jnp.zeros((), bf16))
    lead[:, :wide] = masked
    mine[:, :wide] = masked
    shard[...] = master[...].astype(bf16)


def prepare(place, activations, cotangent, token_ids, master, bias):
    rows, wide = activations.shape
    shapes = [(rows, wide + HALF), (rows, wide + 2 * HALF), (rows, HALF), master.shape]
    return pl.pallas_call(
        prepare_kernel,
        out_shape=[jax.ShapeDtypeStruct(shape, bf16) for shape in shapes],
        in_specs=[SMEM, ANY, ANY, VMEM, VMEM, SMEM],
        out_specs=[VMEM] * 4,
        scratch_shapes=[
            pltpu.VMEM((rows, wide), bf16),
            pltpu.VMEM((rows, wide), bf16),
            pltpu.VMEM((wide, rows), bf16),
            pltpu.VMEM((wide, rows), bf16),
            pltpu.SemaphoreType.DMA((2,)),
        ],
        compiler_params=room(18),
        cost_estimate=cost(0, 8 * rows * wide),
    )(place, in_hbm(activations), in_hbm(cotangent), token_ids[:, None], master, bias)


OVER_ROWS = (((0,), (0,)), ((), ()))
OVER_COLUMNS = (((1,), (1,)), ((), ()))


def gradient_kernel(own, mine, beside, lead, diagonal, *refs):
    outs, flipped, gathered = refs[-2 * NX - 1 : -2], refs[-2], refs[-1]
    rows, wide = own.shape[0], outs[0].shape[1]
    acts = (own[...], beside[:, wide:], lead[:, wide : wide + HALF], diagonal[:, wide + HALF :])
    for i, act in enumerate(acts):
        flipped[:, i * rows : (i + 1) * rows] = act.T
    tile = gathered.shape[1]
    for k in range(wide // tile):
        cols = slice(k * tile, (k + 1) * tile)
        for i, grad in enumerate((mine, beside, lead, diagonal)):
            gathered[i * rows : (i + 1) * rows, :] = grad[:, cols]
        total = jnp.dot(flipped[...], gathered[...], preferred_element_type=f32)
        start = 0
        for out in outs:
            out[:, cols] = total[start : start + out.shape[0]].astype(out.dtype)
            start += out.shape[0]


def gradient_blocks(own, mine, beside, lead, diagonal, after):
    rows = own.shape[0]
    wide = mine.shape[1] - HALF
    return pl.pallas_call(
        gradient_kernel,
        out_shape=[jax.ShapeDtypeStruct((PIECE, wide), f32)]
        + [jax.ShapeDtypeStruct((PIECE // 2, wide), bf16)] * (2 * NX - 2),
        in_specs=[VMEM] * 5 + [ANY] * len(after),
        out_specs=[VMEM] * (2 * NX - 1),
        scratch_shapes=[pltpu.VMEM((HALF, 4 * rows), bf16), pltpu.VMEM((4 * rows, wide // 5), bf16)],
        compiler_params=room(10),
        cost_estimate=cost(8 * HALF * rows * wide, 10_000_000),
    )(own, mine, beside, lead, diagonal, *after)


def join_kernel(*refs):
    for left, right, out in zip(refs[0:2], refs[2:4], refs[4:6]):
        out[...] = (left[...].astype(f32) + right[...].astype(f32)).astype(bf16)


def join(ours, arrived):
    shape = ours[0].shape
    return pl.pallas_call(
        join_kernel,
        out_shape=[jax.ShapeDtypeStruct(shape, bf16)] * 2,
        in_specs=[VMEM] * 4,
        out_specs=[VMEM] * 2,
        compiler_params=room(6),
        cost_estimate=cost(2 * shape[0] * shape[1], 12 * shape[0] * shape[1]),
    )(*ours, *arrived)


def fetch(shards, gathered, sems):
    copies = []
    start = 0
    for i, shard in enumerate(shards):
        to = gathered.at[pl.ds(start, shard.shape[0]), :]
        copies.append(pltpu.make_async_copy(shard, to, sems.at[i]))
        start += shard.shape[0]
    for copy in copies:
        copy.start()
    for copy in copies:
        copy.wait()


def times_weights(flipped, gathered):
    return lax.dot_general(flipped, gathered, (((0,), (0,)), ((), ())), preferred_element_type=f32)


def output_kernel(count, lead, *refs):
    shards, (theirs, gathered) = refs[:count], refs[-2:]
    for i, shard in enumerate(shards):
        gathered[i * PIECE : (i + 1) * PIECE, :] = shard[...]
    theirs[...] = jnp.dot(lead[...], gathered[...], preferred_element_type=f32).astype(bf16)


def output_part(lead, weights, after):
    depth = 2 * HALF
    rows = lead.shape[0]
    wide = weights[0].shape[1]
    steps = 5
    tile = wide // steps
    return pl.pallas_call(
        partial(output_kernel, len(weights)),
        grid=(steps,),
        out_shape=jax.ShapeDtypeStruct((rows, wide), bf16),
        in_specs=[pl.BlockSpec((rows, depth), lambda i: (0, wide // depth))]
        + [pl.BlockSpec((PIECE, tile), lambda i: (0, i))] * len(weights)
        + [ANY] * len(after),
        out_specs=pl.BlockSpec((rows, tile), lambda i: (0, i)),
        scratch_shapes=[pltpu.VMEM((depth, tile), bf16)],
        compiler_params=room(12),
        cost_estimate=cost(2 * depth * rows * wide, 2 * depth * wide + 4 * rows * wide),
    )(lead, *weights, *after)


def products_kernel(count, mine, lead, own, *refs):
    shards = refs[:count]
    theirs, ours, base, gathered, sems = refs[-5:]
    fetch(shards, gathered, sems)
    wide = base.shape[1]
    for out, grad in ((theirs, lead), (ours, mine)):
        back = lax.dot_general(gathered[...], grad[:, :wide], OVER_COLUMNS, preferred_element_type=f32)
        out[...] = back.astype(bf16)
    total = jnp.dot(own[...], gathered[:HALF, :], preferred_element_type=f32)
    base[...] = total + jnp.dot(mine[:, wide:], gathered[HALF:, :], preferred_element_type=f32)


def products(mine, lead, own, weights, after):
    depth = 2 * HALF
    rows = own.shape[0]
    wide = weights[0].shape[1]
    return pl.pallas_call(
        partial(products_kernel, len(weights)),
        out_shape=[jax.ShapeDtypeStruct((depth, rows), bf16)] * 2 + [jax.ShapeDtypeStruct((rows, wide), f32)],
        in_specs=[VMEM] * 3 + [ANY] * (len(weights) + len(after)),
        out_specs=[VMEM] * 3,
        scratch_shapes=[pltpu.VMEM((depth, wide), bf16), pltpu.SemaphoreType.DMA((len(weights),))],
        compiler_params=room(16),
        cost_estimate=cost(6 * depth * rows * wide, 2 * depth * wide + 10 * rows * wide),
    )(mine, lead, own, *weights, *after)


def adam_kernel(bias, master, first, second, here, *refs):
    low, high = refs[0:2], refs[2:4]
    stepped, sent, first_out, second_out = refs[-4:]

    def update(arrived):
        gradient = here[...]
        for part in arrived:
            gradient += part[...].astype(f32)
        rows = master[...]
        first_new = beta_one * first[...].astype(f32) + (1.0 - beta_one) * gradient
        second_new = beta_two * second[...].astype(f32) + (1.0 - beta_two) * gradient * gradient
        first_hat = first_new / bias[0]
        second_hat = second_new / bias[1]
        delta = learn_rate * (first_hat / (jnp.sqrt(second_hat) + epsilon) + decay_rate * rows)
        stepped[...] = rows - delta
        sent[...] = (rows - delta).astype(bf16)
        first_out[...] = first_new.astype(bf16)
        second_out[...] = second_new.astype(bf16)

    first_half = pl.program_id(0) < pl.num_programs(0) // 2

    @pl.when(first_half)
    def _():
        update(low)

    @pl.when(jnp.logical_not(first_half))
    def _():
        update(high)


def adam(bias, master, first, second, here, low, high):
    rows, wide = master.shape
    steps = 2
    turn = steps // 2
    part = pl.BlockSpec((rows // steps, wide), lambda i: (i, 0))
    lows = pl.BlockSpec((rows // steps, wide), lambda i: (jnp.minimum(i, turn - 1), 0))
    highs = pl.BlockSpec((rows // steps, wide), lambda i: (jnp.maximum(i - turn, 0), 0))
    return pl.pallas_call(
        adam_kernel,
        grid=(steps,),
        out_shape=[jax.ShapeDtypeStruct((rows, wide), f32)] + [jax.ShapeDtypeStruct((rows, wide), bf16)] * 3,
        in_specs=[SMEM] + [part] * 4 + [lows] * 2 + [highs] * 2,
        out_specs=[part] * 4,
        compiler_params=room(18),
        cost_estimate=cost(20 * rows * wide, 26 * rows * wide),
    )(bias, master, first, second, here, *low, *high)


def finish_kernel(place, ours, base, theirs, arrived, stepped, other, output, act_grad, averaged, *scratch):
    ordered, ours_here, base_here, sems = scratch
    h = place[1]
    step = pl.program_id(0)
    steps, _, width = base_here.shape
    loads = [
        pltpu.make_async_copy(base.at[:, i * width : (i + 1) * width], base_here.at[i], sems.at[i])
        for i in range(steps)
    ]

    @pl.when(step == 0)
    def _():
        load = pltpu.make_async_copy(ours, ours_here, sems.at[steps])
        load.start()
        for part in loads:
            part.start()
        load.wait()
        for slot in range(2):
            for j in range(NX):
                start = slot * HALF + j * PIECE
                piece = slice(start, start + PIECE)
                ordered[pl.ds(row_of(place, h, slot, j), PIECE), :] = ours_here[piece, :]
                ordered[pl.ds(row_of(place, 1 - h, slot, j), PIECE), :] = theirs[piece, :]

    act_grad[...] = ordered[pl.ds(pl.multiple_of(step * width, width), width), :].T
    averaged[...] = 0.5 * (stepped[...] + other[...].astype(f32))
    for i in range(steps):

        @pl.when(step == i)
        def _():
            loads[i].wait()
            output[...] = (base_here[i] + arrived[...].astype(f32)).astype(bf16)


def finish(place, ours, theirs, base, arrived, stepped, other):
    rows, wide = base.shape
    depth = ours.shape[0]
    mine = stepped.shape[0]
    steps = 5
    cols = pl.BlockSpec((rows, wide // steps), lambda i: (0, i))
    part = pl.BlockSpec((mine // steps, wide), lambda i: (i, 0))
    whole = pl.BlockSpec((depth, rows), lambda i: (0, 0))
    return pl.pallas_call(
        finish_kernel,
        grid=(steps,),
        out_shape=[
            jax.ShapeDtypeStruct((rows, wide), bf16),
            jax.ShapeDtypeStruct((rows, 2 * depth), bf16),
            jax.ShapeDtypeStruct((mine, wide), f32),
        ],
        in_specs=[SMEM, ANY, ANY, whole, cols, part, part],
        out_specs=[cols, cols, part],
        scratch_shapes=[
            pltpu.VMEM((2 * depth, rows), bf16),
            pltpu.VMEM((depth, rows), bf16),
            pltpu.VMEM((steps, rows, wide // steps), f32),
            pltpu.SemaphoreType.DMA((steps + 1,)),
        ],
        compiler_params=room(18),
        cost_estimate=cost(4 * rows * wide, 18 * rows * wide),
    )(place, in_hbm(ours), in_hbm(base), theirs, arrived, stepped, other)


def from_partner(value, bit_index):
    mask = 2**bit_index
    pairs = [(source, source ^ mask) for source in range(lax.axis_size("group"))]
    return lax.ppermute(value, "group", pairs)


def exchange(sent, beside, bit_index):
    levels = lax.axis_size("group").bit_length() - 1

    def branch(level, value, rest):
        return from_partner(value, level), [send(part, pairs) for part, pairs in zip(rest, moves)]

    rest, moves = [part for part, _ in beside], [pairs for _, pairs in beside]
    return lax.switch(bit_index, [partial(branch, level) for level in range(levels)], sent, rest)


def shards(activations, cotangent, token_ids, step_count, master, first_moment, second_moment):
    master, first_old, second_old = master[0], first_moment[0], second_moment[0]
    levels = lax.axis_size("group").bit_length() - 1
    bit_index = step_count[0] % levels
    f = lax.axis_index("fsdp")
    place = jnp.stack([f // 4, (f // 2) % 2, f % 2]).astype(jnp.int32)
    steps_done = (step_count[0] + 1).astype(f32)
    bias = jnp.stack([1.0 - jnp.power(f32(beta_one), steps_done), 1.0 - jnp.power(f32(beta_two), steps_done)])

    mine, lead, own, shard = prepare(place, activations, cotangent, token_ids, master, bias)
    lead, beside = send(lead, ACROSS), send(mine, SIBLING)
    pieces = [shard, send(shard, PREV), send(shard, OPPOSITE), send(shard, NEXT)]
    weights = pieces + [send(part, SIBLING) for part in pieces]
    lead = held_until(lead, [*weights[NX:], beside])
    output = output_part(lead, weights, [])
    blocks = gradient_blocks(own, mine, beside, lead, send(lead, SIBLING), [output])
    output = send(output, ACROSS)
    here, next_low, next_high, far_low, far_high, prev_low, prev_high = blocks
    next_low, prev_high = join((next_low, prev_high), (send(far_low, NEXT), send(far_high, PREV)))
    low = [send(next_low, NEXT), send(prev_low, PREV)]
    high = [send(next_high, NEXT), send(prev_high, PREV)]
    theirs, ours, base = products(mine, lead, own, weights, [next_low])
    stepped, sent, first_out, second_out = adam(bias, master, first_old, second_old, here, low, high)
    arrived, (theirs,) = exchange(sent, [(theirs, ACROSS)], bit_index)
    output, act_grad, averaged = finish(place, ours, theirs, base, output, stepped, arrived)
    return (output, act_grad, averaged[None], first_out[None], second_out[None])


def solution(mesh):
    rows = P(("group", "fsdp"), None)
    state = P("group", "fsdp", None)
    return jax.shard_map(
        shards,
        mesh=mesh,
        in_specs=(rows, rows, P(("group", "fsdp")), P(), state, state, state),
        out_specs=(rows, rows, state, state, state),
        check_vma=False,
    )
```
